256 devices in a mesh: win: 8 (over z_lo, x), tile: 32 (over y, z_hi, core).
Axes of the slice: x: 4, y: 4, z: 8 (z_hi: 4, z_lo: 2; z = z_hi * 2 + z_lo), core: 2. Of those that a mesh axis runs over, the one named last changes fastest.
Arguments:
- adjoint: float32 [8, 4, 32, 512, 320], P('win', None, None, 'tile'), may hold values from -6 to 6
- velocity: float32 [8, 2, 2, 32, 512, 320], P('win', None, None, None, 'tile'), may hold values from -0.5 to 0.5
- kappa: float32 [8, 2, 32, 512, 320], P('win', None, None, 'tile'), may hold values from 0.02 to 0.2
Outputs:
- result: float32 [8, 4, 32, 512, 320], P('win', None, None, 'tile')
The draws below stay inside these ranges and needn't reach their ends.
All inputs are finite; a program needn't handle non-finite values.
Results may differ from the reference program's by a relative error of at most 0.00002.
Values sent between devices are 32-bit elements; how exact they have to be, the bound alone decides.
No kernel may reach another device: no remote copies, remote signals or barrier semaphores. Data moves between devices by JAX's collectives and lax.ppermute only.
A program may use at most 128 MiB of HBM per device.

```python
import math
import jax
import jax.numpy as jnp
from jax import lax

FIELDS = 4
LEV = 32
NLAT = 320
STEPS = 2
NLON = 512
WINDOWS = 8


def shard_levels(key, dims, shards, least, largest):
    def one(position, shards_of):
        heights = jax.random.uniform(jax.random.fold_in(jax.random.fold_in(key, 6), position), (shards_of,), jnp.float32, least / len(shards), largest / len(shards))
        return jnp.repeat(jnp.exp(heights), dims[position] // shards_of).reshape((-1,) + (1,) * (len(dims) - position - 1))

    loudness = one(*shards[0])
    for cut in shards[1:]:
        loudness = loudness * one(*cut)
    return loudness


def centred(rng, dims, deviation, limit, shards=(), held_as=jnp.bfloat16):
    result = deviation * jax.random.normal(rng, dims, jnp.float32)
    if shards:
        result = result * shard_levels(rng, dims, shards, -0.22, 0.18)
    return jnp.clip(result, -limit, limit).astype(held_as)


def setup_inputs(seed: int = 0) -> dict:
    splits = jax.random.split(jax.random.key(seed), 4)
    adjoint = centred(splits[0], (WINDOWS, FIELDS, LEV, NLON, NLAT), 1.0, 6.0, ((0, 8), (3, 32)), jnp.float32)
    velocity = jnp.clip(jax.random.uniform(splits[1], (WINDOWS, STEPS, 2, LEV, NLON, NLAT), jnp.float32, -0.5, 0.5) * shard_levels(splits[1], (WINDOWS, STEPS, 2, LEV, NLON, NLAT), ((0, 8), (4, 32)), -0.4, 0.0), -0.5, 0.5)
    kappa = jnp.clip(jnp.exp(math.log(0.2) - 2.3025851 * jax.random.uniform(splits[2], (WINDOWS, STEPS, LEV, NLON, NLAT), jnp.float32) ** shard_levels(splits[2], (WINDOWS, STEPS, LEV, NLON, NLAT), ((0, 8), (3, 32)), -0.2, 0.2)), 0.02, 0.2)
    return dict(adjoint=adjoint, velocity=velocity, kappa=kappa)


def lat_pair(field):
    edge = jnp.zeros_like(field[..., :1])
    upper = jnp.concatenate([field[..., 1:], edge], axis=-1)
    lower = jnp.concatenate([edge, field[..., :-1]], axis=-1)
    return upper, lower


def adjoint_step(state, along_rate, across_rate, spread_rate):
    carried = along_rate * state
    spread = spread_rate * state
    lateral = across_rate * state
    along = (8.0 * (jnp.roll(carried, -1, 2) - jnp.roll(carried, 1, 2)) - (jnp.roll(carried, -2, 2) - jnp.roll(carried, 2, 2))) / 12.0
    lat_up, lat_down = lat_pair(lateral)
    spread_up, spread_down = lat_pair(spread)
    diffuse = jnp.roll(spread, -1, 2) + jnp.roll(spread, 1, 2) + spread_up + spread_down - 4.0 * spread
    return state + along + 0.5 * (lat_up - lat_down) + diffuse


def window_image(inputs):
    state, velocity, kappa = inputs
    for section in range(STEPS - 1, -1, -1):
        state = adjoint_step(state, velocity[section, 0], velocity[section, 1], kappa[section])
    return state


def reference(adjoint, velocity, kappa):
    images = lax.map(window_image, (adjoint, velocity, kappa))
    later = jnp.concatenate([images[1:], jnp.zeros_like(images[:1])], axis=0)
    return adjoint - later
```

```python
import functools

import jax
import jax.numpy as jnp
from jax import lax
from jax.experimental import pallas as pl
from jax.experimental.pallas import tpu as pltpu
from jax.sharding import PartitionSpec as P

FIELDS, LON, LAT = 4, 16, 320
WIDE = 384
BLOCK = 4
CHUNKS = ((0, 8), (8, 12), (20, 12))


def wide(x):
    return jnp.concatenate([x, jnp.zeros((x.shape[0], WIDE - LAT), x.dtype)], axis=1)


def ends(x):
    row = lax.broadcasted_iota(jnp.int32, (8, x.shape[1]), 0)
    return jnp.where(row < 4, x[0:8], x[8:16])


def middle(x):
    row = lax.broadcasted_iota(jnp.int32, (8, x.shape[1]), 0)
    return jnp.where(row < 4, x[8:16], x[0:8])


def rates(a, b, c):
    along = a * (2.0 / 3.0)
    across = b * 0.5
    return dict(
        centre=1.0 - 4.0 * c,
        down=c + along,
        up=c - along,
        far=a * (1.0 / 12.0),
        lat_down=c + across,
        lat_up=c - across,
    )


def rolled(x, shift, axis):
    size = x.shape[axis]
    return pltpu.roll(x, shift % size, axis)


def inside(r, first, last):
    row = lax.broadcasted_iota(jnp.int32, r["far"].shape, 0)
    return dict(
        centre=r["centre"],
        lat_down=r["lat_down"],
        lat_up=r["lat_up"],
        down=jnp.where(row > first, r["down"], 0.0),
        up=jnp.where(row < last, r["up"], 0.0),
        far_down=jnp.where(row > first + 1, r["far"], 0.0),
        far_up=jnp.where(row < last - 1, r["far"], 0.0),
    )


def step(w, r):
    out = r["centre"] * w
    out += rolled(r["down"] * w, -1, 0) + rolled(r["up"] * w, 1, 0)
    out += rolled(r["far_up"] * w, 2, 0) - rolled(r["far_down"] * w, -2, 0)
    out += rolled(r["lat_down"] * w, -1, 1) + rolled(r["lat_up"] * w, 1, 1)
    return out


def leaving_rates(r):
    row = lax.broadcasted_iota(jnp.int32, r["far"].shape, 0)
    return dict(
        down=jnp.where(row == 0, r["down"], 0.0),
        up=jnp.where(row == 7, r["up"], 0.0),
        far_down=jnp.where(row < 2, r["far"], 0.0),
        far_up=jnp.where(row >= 6, r["far"], 0.0),
    )


def leaving(ws, r):
    to_next = 0.0
    to_previous = 0.0
    for f, w in enumerate(ws):
        to_next += rolled(r["up"] * w, 2 * f + 1, 0) + rolled(r["far_up"] * w, 2 * f + 2, 0)
        to_previous += rolled(r["down"] * w, 2 * f + 1, 0) - rolled(r["far_down"] * w, 2 * f, 0)
    return to_next, to_previous


def arriving(from_previous, from_next, f):
    row = lax.broadcasted_iota(jnp.int32, from_next.shape, 0)
    low = jnp.where(row < 2, rolled(from_previous, -2 * f, 0), 0.0)
    return jnp.where(row >= 6, rolled(from_next, 6 - 2 * f, 0), low)


def put_packed(ref, l, pieces):
    lane = lax.broadcasted_iota(jnp.int32, (8, 128), 1)
    for pair in range(FIELDS // 2):
        first, second = pieces[2 * pair], pieces[2 * pair + 1]
        base = 40 * pair
        ref[l, base : base + 8] = first[:, 0:128]
        ref[l, base + 8 : base + 16] = first[:, 128:256]
        ref[l, base + 16 : base + 24] = second[:, 0:128]
        ref[l, base + 24 : base + 32] = second[:, 128:256]
        ref[l, base + 32 : base + 40] = jnp.where(
            lane < 64, first[:, 256:384], pltpu.roll(second[:, 256:384], 64, 1)
        )


def get_packed(ref, l, f, part):
    base = 40 * (f // 2)
    if part < 2:
        at = base + 16 * (f % 2) + 8 * part
        return ref[l, at : at + 8]
    last = ref[l, base + 32 : base + 40]
    return pltpu.roll(last, 64, 1) if f % 2 else last


def levels(body):
    pl.loop(0, BLOCK)(body)


def first_kernel(adj, vel, kap, mid, image, state, to_next, to_previous):
    @levels
    def _(l):
        ws = [wide(adj[f, l]) for f in range(FIELDS)]
        for s in (1, 0):
            r = rates(wide(vel[s, 0, l]), wide(vel[s, 1, l]), wide(kap[s, l]))
            if s == 1:
                out = leaving_rates({k: ends(v) for k, v in r.items() if k in ("down", "up", "far")})
                to_next[l], to_previous[l] = leaving([ends(w) for w in ws], out)
            r = inside(r, 0, LON - 1)
            ws = [step(w, r) for w in ws]
            if s == 1:
                for f, w in enumerate(ws):
                    state[l, f] = ends(w)
        put_packed(mid, l, [middle(w) for w in ws])
        for f, w in enumerate(ws):
            image[l, f] = ends(w)


def second_kernel(vel, kap, from_previous, from_next, state, image, image_out, to_next, to_previous):
    @levels
    def _(l):
        r = rates(wide(ends(vel[0, 0, l])), wide(ends(vel[0, 1, l])), wide(ends(kap[0, l])))
        low, high = from_previous[l], from_next[l]
        new = [arriving(low, high, f) for f in range(FIELDS)]
        to_next[l], to_previous[l] = leaving([state[l, f] + new[f] for f in range(FIELDS)], leaving_rates(r))
        r = inside(r, 0, 7)
        for f in range(FIELDS):
            image_out[l, f] = image[l, f] + step(new[f], r)


def third_kernel(from_previous, from_next, image, packed):
    @levels
    def _(l):
        low, high = from_previous[l], from_next[l]
        put_packed(packed, l, [image[l, f] + arriving(low, high, f) for f in range(FIELDS)])


def last_kernel(adj, mid, end, *refs):
    out = refs[-1]
    row = lax.broadcasted_iota(jnp.int32, (8, 128), 0)

    @levels
    def _(l):
        for f in range(FIELDS):
            for part in range(3):
                lanes = slice(128 * part, min(128 * part + 128, LAT))
                n = lanes.stop - lanes.start
                m, e = get_packed(mid, l, f, part), get_packed(end, l, f, part)
                out[f, l, 0:8, lanes] = adj[f, l, 0:8, lanes] - jnp.where(row < 4, e, m)[:, :n]
                out[f, l, 8:16, lanes] = adj[f, l, 8:16, lanes] - jnp.where(row < 4, m, e)[:, :n]


def spec(dims, at, first=0):
    block = tuple(BLOCK if i == at else d for i, d in enumerate(dims))
    return pl.BlockSpec(block, lambda i: tuple(first + i if k == at else 0 for k in range(len(dims))))


def f32(*dims):
    return jax.ShapeDtypeStruct(dims, jnp.float32)


def call(kernel, count, in_specs, out_specs, out_shape, name, cost, **kw):
    return pl.pallas_call(
        kernel,
        grid=(count // BLOCK,),
        in_specs=in_specs,
        out_specs=out_specs,
        out_shape=out_shape,
        name=name,
        cost_estimate=pl.CostEstimate(flops=cost * count, bytes_accessed=cost * count, transcendentals=0),
        compiler_params=pltpu.CompilerParams(vmem_limit_bytes=48 * 1024 * 1024),
        **kw,
    )


TILE = (0, 8, WIDE)
FIELD_TILES = (0, FIELDS, 8, WIDE)
PACKED = (0, 80, 128)


def sized(dims, n):
    return f32(n, *dims[1:])


def neighbours(to_next, to_previous):
    n = lax.axis_size("tile")
    ahead = [(i, (i + 1) % n) for i in range(n)]
    back = [(j, i) for i, j in ahead]
    return lax.ppermute(to_next, "tile", ahead), lax.ppermute(to_previous, "tile", back)


def to_preceding(x):
    n = lax.axis_size("win")
    return lax.ppermute(x, "win", [(k + 1, k) for k in range(n - 1)])


def per_device(adjoint, velocity, kappa):
    adj, vel, kap = adjoint[0], velocity[0], kappa[0]
    lev = adj.shape[1]
    adj_dims, vel_dims, kap_dims = adj.shape, vel.shape, kap.shape
    firsts = []
    for start, n in CHUNKS:
        b = start // BLOCK
        mid, image, state, to_next, to_previous = call(
            first_kernel, n,
            [spec(adj_dims, 1, b), spec(vel_dims, 2, b), spec(kap_dims, 1, b)],
            [spec(PACKED, 0), spec(FIELD_TILES, 0), spec(FIELD_TILES, 0), spec(TILE, 0), spec(TILE, 0)],
            [sized(PACKED, n), sized(FIELD_TILES, n), sized(FIELD_TILES, n), sized(TILE, n), sized(TILE, n)],
            "interior", 250000,
        )(adj, vel, kap)
        firsts.append((to_preceding(mid), image, state, neighbours(to_next, to_previous)))
    seconds = []
    for (start, n), (mid, image, state, (low, high)) in zip(CHUNKS, firsts):
        b = start // BLOCK
        image, to_next, to_previous = call(
            second_kernel, n,
            [spec(vel_dims, 2, b), spec(kap_dims, 1, b), spec(TILE, 0), spec(TILE, 0), spec(FIELD_TILES, 0), spec(FIELD_TILES, 0)],
            [spec(FIELD_TILES, 0), spec(TILE, 0), spec(TILE, 0)],
            [sized(FIELD_TILES, n), sized(TILE, n), sized(TILE, n)],
            "ends_first", 100000,
        )(vel, kap, low, high, state, image)
        seconds.append((mid, image, neighbours(to_next, to_previous)))
    thirds = []
    for (start, n), (mid, image, (low, high)) in zip(CHUNKS, seconds):
        end = call(
            third_kernel, n,
            [spec(TILE, 0), spec(TILE, 0), spec(FIELD_TILES, 0)],
            spec(PACKED, 0), sized(PACKED, n), "ends_second", 50000,
        )(low, high, image)
        thirds.append((mid, to_preceding(end)))
    out = None
    for (start, n), (mid, end) in zip(CHUNKS, thirds):
        b = start // BLOCK
        more = {} if out is None else dict(input_output_aliases={3: 0})
        args = () if out is None else (out,)
        out = call(
            last_kernel, n,
            [spec(adj_dims, 1, b), spec(PACKED, 0), spec(PACKED, 0)] + [pl.BlockSpec(memory_space=pl.ANY)] * len(args),
            spec(adj_dims, 1, b), f32(*adj_dims), "subtract", 80000, **more,
        )(adj, mid, end, *args)
    return out[None]


def solution(mesh):
    return jax.shard_map(
        per_device,
        mesh=mesh,
        in_specs=(
            P("win", None, None, "tile", None),
            P("win", None, None, None, "tile", None),
            P("win", None, None, "tile", None),
        ),
        out_specs=P("win", None, None, "tile", None),
        check_vma=False,
    )
```

```python
import functools

import jax
import jax.numpy as jnp
from jax import lax
from jax.experimental import pallas as pl
from jax.experimental.pallas import tpu as pltpu
from jax.sharding import PartitionSpec as P

FIELDS, LON, LAT = 4, 16, 320
WIDE = 384
BLOCK = 4
FLOPS = 2000000000
FIRST_VMEM = 54
MIB = 1024 * 1024
HALVES = ((0, 16, ((0, 8), (8, 8))), (16, 16, ((16, 16),)))


def wide(x):
    return jnp.concatenate([x, jnp.zeros((x.shape[0], WIDE - LAT), x.dtype)], axis=1)


def ends(x):
    row = lax.broadcasted_iota(jnp.int32, (8, x.shape[1]), 0)
    return jnp.where(row < 4, x[0:8], x[8:16])


def middle(x):
    row = lax.broadcasted_iota(jnp.int32, (8, x.shape[1]), 0)
    return jnp.where(row < 4, x[8:16], x[0:8])


def rates(a, b, c):
    along = a * (2.0 / 3.0)
    across = b * 0.5
    return dict(
        centre=1.0 - 4.0 * c,
        down=c + along,
        up=c - along,
        far=a * (1.0 / 12.0),
        lat_down=c + across,
        lat_up=c - across,
    )


def rolled(x, shift, axis):
    size = x.shape[axis]
    return pltpu.roll(x, shift % size, axis)


def inside(r, first, last):
    row = lax.broadcasted_iota(jnp.int32, r["far"].shape, 0)
    return dict(
        centre=r["centre"],
        lat_down=r["lat_down"],
        lat_up=r["lat_up"],
        down=jnp.where(row > first, r["down"], 0.0),
        up=jnp.where(row < last, r["up"], 0.0),
        far_down=jnp.where(row > first + 1, r["far"], 0.0),
        far_up=jnp.where(row < last - 1, r["far"], 0.0),
    )


def step(w, r):
    out = r["centre"] * w
    out += rolled(r["down"] * w, -1, 0) + rolled(r["up"] * w, 1, 0)
    out += rolled(r["far_up"] * w, 2, 0) - rolled(r["far_down"] * w, -2, 0)
    out += rolled(r["lat_down"] * w, -1, 1) + rolled(r["lat_up"] * w, 1, 1)
    return out


def leaving_rates(r):
    row = lax.broadcasted_iota(jnp.int32, r["far"].shape, 0)
    return dict(
        down=jnp.where(row == 0, r["down"], 0.0),
        up=jnp.where(row == 7, r["up"], 0.0),
        far_down=jnp.where(row < 2, r["far"], 0.0),
        far_up=jnp.where(row >= 6, r["far"], 0.0),
    )


def leaving(ws, r):
    to_next = 0.0
    to_previous = 0.0
    for f, w in enumerate(ws):
        to_next += rolled(r["up"] * w, 2 * f + 1, 0) + rolled(r["far_up"] * w, 2 * f + 2, 0)
        to_previous += rolled(r["down"] * w, 2 * f + 1, 0) - rolled(r["far_down"] * w, 2 * f, 0)
    return to_next, to_previous


def arriving(from_previous, from_next, f):
    row = lax.broadcasted_iota(jnp.int32, from_next.shape, 0)
    low = jnp.where(row < 2, rolled(from_previous, -2 * f, 0), 0.0)
    return jnp.where(row >= 6, rolled(from_next, 6 - 2 * f, 0), low)


def put_pair(ref, l, base, first, second):
    lane = lax.broadcasted_iota(jnp.int32, (8, 128), 1)
    ref[l, base : base + 8] = first[:, 0:128]
    ref[l, base + 8 : base + 16] = first[:, 128:256]
    ref[l, base + 16 : base + 24] = second[:, 0:128]
    ref[l, base + 24 : base + 32] = second[:, 128:256]
    ref[l, base + 32 : base + 40] = jnp.where(
        lane < 64, first[:, 256:384], pltpu.roll(second[:, 256:384], 64, 1)
    )


def put_packed(ref, l, pieces):
    for pair in range(FIELDS // 2):
        put_pair(ref, l, 40 * pair, pieces[2 * pair], pieces[2 * pair + 1])


def get_packed(ref, l, f, part):
    base = 40 * (f // 2)
    if part < 2:
        at = base + 16 * (f % 2) + 8 * part
        return ref[l, at : at + 8]
    last = ref[l, base + 32 : base + 40]
    return pltpu.roll(last, 64, 1) if f % 2 else last


def levels(body):
    pl.loop(0, BLOCK)(body)


def put_message(ref, l, now, then, r):
    put_pair(ref, l, 0, now, then)
    row = lax.broadcasted_iota(jnp.int32, (8, 128), 0)
    last = r[:, 256:384]
    rest = pltpu.roll(jnp.where(row < 2, last, 0.0), 6, 0)
    rest += pltpu.roll(pltpu.roll(jnp.where(row == 2, last, 0.0), 64, 1), 4, 0)
    ref[l, 40:48] = r[:, 0:128] + pltpu.roll(r[:, 128:256], 3, 0) + rest


def get_rate(message, k):
    last = message[46 + k % 2 : 47 + k % 2]
    if k == 2:
        last = pltpu.roll(jnp.broadcast_to(last, (8, 128)), 64, 1)
    parts = [message[40 + k : 41 + k], message[43 + k : 44 + k], last]
    return jnp.concatenate([jnp.broadcast_to(p, (8, 128)) for p in parts], axis=1)


def get_tile(message, k):
    base = 16 * k
    last = message[32:40]
    if k == 1:
        last = pltpu.roll(last, 64, 1)
    return jnp.concatenate([message[base : base + 8], message[base + 8 : base + 16], last], axis=1)


def leaving_rows(r):
    to_next = rolled(r["far_up"], 2, 0) + rolled(r["up"], 3, 0)
    to_previous = r["far_down"] + rolled(r["down"], 2, 0)
    return to_next, to_previous


def odd_tile():
    return lax.axis_index("tile") % 2 == 1


def first_kernel(base, adj, vel, kap, *refs):
    mid, image, partner, other, adj_buf, vel_buf, kap_buf, sem = refs[-8:]
    at, count = pl.program_id(0), pl.num_programs(0)

    def copies(block):
        slot = block % 2
        rows = pl.ds(base + block * BLOCK, BLOCK)
        return [
            pltpu.make_async_copy(adj.at[:, rows], adj_buf.at[slot], sem.at[slot, 0]),
            pltpu.make_async_copy(vel.at[:, :, rows], vel_buf.at[slot], sem.at[slot, 1]),
            pltpu.make_async_copy(kap.at[:, rows], kap_buf.at[slot], sem.at[slot, 2]),
        ]

    @pl.when(at == 0)
    def _():
        for copy in copies(at):
            copy.start()

    @pl.when(at + 1 < count)
    def _():
        for copy in copies(at + 1):
            copy.start()

    for copy in copies(at):
        copy.wait()
    adj, vel, kap = adj_buf.at[at % 2], vel_buf.at[at % 2], kap_buf.at[at % 2]

    @levels
    def _(l):
        odd = odd_tile()
        ws = [wide(adj[f, l]) for f in range(FIELDS)]
        sent = []
        for s in (1, 0):
            r = rates(wide(vel[s, 0, l]), wide(vel[s, 1, l]), wide(kap[s, l]))
            out = leaving_rates({k: ends(v) for k, v in r.items() if k in ("down", "up", "far")})
            sent.append(leaving([ends(w) for w in ws], out))
            r = inside(r, 0, LON - 1)
            ws = [step(w, r) for w in ws]
        sent.append(leaving_rows(out))
        put_message(partner, l, *[jnp.where(odd, p, n) for n, p in sent])
        put_message(other, l, *[jnp.where(odd, n, p) for n, p in sent])
        put_packed(mid, l, [middle(w) for w in ws])
        for f, w in enumerate(ws):
            image[l, f] = ends(w)


def second_kernel(vel, kap, partner, other, from_partner, from_other, image, *refs):
    packed = refs[-1]

    @levels
    def _(l):
        odd = odd_tile()
        row = lax.broadcasted_iota(jnp.int32, (8, WIDE), 0)
        even_row = row % 2 == 0
        sides = []
        for (mine_even, mine_odd), (theirs_even, theirs_odd) in (
            ((other, partner), (from_other, from_partner)),
            ((partner, other), (from_partner, from_other)),
        ):
            mine = jnp.where(odd, mine_odd[l], mine_even[l])
            theirs = jnp.where(odd, theirs_odd[l], theirs_even[l])
            sides.append((get_tile(mine, 0), get_tile(theirs, 0), get_tile(theirs, 1), theirs))
        gave, low, low_then, theirs = sides[0]
        low_then += jnp.where(even_row, get_rate(theirs, 0), get_rate(theirs, 1)) * gave
        low_then += jnp.where(even_row, get_rate(theirs, 2) * rolled(gave, -1, 0), 0.0)
        gave, high, high_then, theirs = sides[1]
        high_then -= jnp.where(even_row, get_rate(theirs, 0), get_rate(theirs, 1)) * gave
        high_then += jnp.where(even_row, 0.0, get_rate(theirs, 2) * rolled(gave, 1, 0))
        r = rates(wide(ends(vel[0, 0, l])), wide(ends(vel[0, 1, l])), wide(ends(kap[0, l])))
        r = inside(r, 0, 7)
        pieces = []
        for f in range(FIELDS):
            new = arriving(low, high, f)
            pieces.append(image[l, f] + step(new, r) + arriving(low_then, high_then, f))
        put_packed(packed, l, pieces)


def last_kernel(adj, mid, mid_late, end, *refs):
    out = refs[-1]
    win, windows = lax.axis_index("win"), lax.axis_size("win")
    late, none = win == windows // 2 - 1, win == windows - 1
    row = lax.broadcasted_iota(jnp.int32, (8, 128), 0)

    @levels
    def _(l):
        for f in range(FIELDS):
            for part in range(3):
                lanes = slice(128 * part, min(128 * part + 128, LAT))
                n = lanes.stop - lanes.start
                m = jnp.where(late, get_packed(mid_late, l, f, part), get_packed(mid, l, f, part))
                m = jnp.where(none, 0.0, m)
                e = get_packed(end, l, f, part)
                out[f, l, 0:8, lanes] = adj[f, l, 0:8, lanes] - jnp.where(row < 4, e, m)[:, :n]
                out[f, l, 8:16, lanes] = adj[f, l, 8:16, lanes] - jnp.where(row < 4, m, e)[:, :n]


def spec(dims, at, first=0):
    block = tuple(BLOCK if i == at else d for i, d in enumerate(dims))
    return pl.BlockSpec(block, lambda i: tuple(first + i if k == at else 0 for k in range(len(dims))))


def f32(*dims):
    return jax.ShapeDtypeStruct(dims, jnp.float32)


def call(kernel, count, in_specs, out_specs, out_shape, name, args, after=(), into=(), scratch=(), vmem=24):
    args, in_specs, aliases = list(args), list(in_specs), {}
    for extra in after:
        args.append(extra)
        in_specs.append(pl.BlockSpec(memory_space=pl.ANY))
    for k, buffer in enumerate(into):
        if buffer is not None:
            aliases[len(args)] = k
            args.append(buffer)
            in_specs.append(pl.BlockSpec(memory_space=pl.ANY))
    return pl.pallas_call(
        kernel,
        grid=(count // BLOCK,),
        in_specs=in_specs,
        out_specs=out_specs,
        out_shape=out_shape,
        scratch_shapes=list(scratch),
        name=name,
        input_output_aliases=aliases,
        cost_estimate=pl.CostEstimate(flops=FLOPS, bytes_accessed=1, transcendentals=0),
        compiler_params=pltpu.CompilerParams(vmem_limit_bytes=vmem * MIB),
    )(*args)


MESSAGE = (0, 48, 128)
FIELD_TILES = (0, FIELDS, 8, WIDE)
PACKED = (0, 80, 128)


def sized(dims, n):
    return f32(n, *dims[1:])


def swapped(partner, other):
    n = lax.axis_size("tile")
    inner = [(i, i ^ 1) for i in range(n)]
    outer = [(i, (i + 1 if i % 2 else i - 1) % n) for i in range(n)]
    return lax.ppermute(partner, "tile", inner), lax.ppermute(other, "tile", outer)


def to_preceding(x, detour=False):
    n = lax.axis_size("win")
    pairs = [(k + 1, k) for k in range(n - 1)]
    if not detour:
        return lax.ppermute(x, "win", pairs)
    first = [(k, n - 1 if k == n // 2 else j) for k, j in pairs]
    arrived = lax.ppermute(x, "win", first)
    return arrived, lax.ppermute(arrived, "win", [(n - 1, n // 2 - 1)])


def per_device(adjoint, velocity, kappa):
    adj, vel, kap = adjoint[0], velocity[0], kappa[0]
    after = []
    mids, halves = [], []
    for start, n, pieces in HALVES:
        into = [None] * 4
        for first, count in pieces:
            c = (first - start) // BLOCK
            outs = call(
                functools.partial(first_kernel, first), count,
                [pl.BlockSpec(memory_space=pltpu.HBM)] * 3,
                [spec(PACKED, 0)] + [spec(d, 0, c) for d in (FIELD_TILES, MESSAGE, MESSAGE)],
                [sized(PACKED, count)] + [sized(d, n) for d in (FIELD_TILES, MESSAGE, MESSAGE)],
                "interior", (adj, vel, kap), after, into,
                [
                    pltpu.VMEM((2, FIELDS, BLOCK, LON, LAT), jnp.float32),
                    pltpu.VMEM((2, 2, 2, BLOCK, LON, LAT), jnp.float32),
                    pltpu.VMEM((2, 2, BLOCK, LON, LAT), jnp.float32),
                    pltpu.SemaphoreType.DMA((2, 3)),
                ],
                FIRST_VMEM,
            )
            into = [None] + list(outs[1:])
            after = [outs[0]]
            mids.append((first, count, *to_preceding(outs[0], True)))
        halves.append((outs[1], outs[2:], swapped(*outs[2:])))
    after = after + [mids[0][2], mids[1][2]]
    ends = []
    for (start, n, _), (image, mine, theirs) in zip(HALVES, halves):
        b = start // BLOCK
        end = call(
            second_kernel, n,
            [spec((1, *vel.shape[1:]), 2, b), spec((1, *kap.shape[1:]), 1, b)] + [spec(d, 0) for d in (MESSAGE,) * 4 + (FIELD_TILES,)],
            spec(PACKED, 0), sized(PACKED, n), "ends", (vel, kap, *mine, *theirs, image), after,
        )
        after = [end, mids[2][2]]
        ends.append((start, n, to_preceding(end)))
    after = [end]
    out = None
    for first, count, mid, mid_late in mids:
        start, end = [(s, e) for s, n, e in ends if s <= first < s + n][0]
        b = first // BLOCK
        out = call(
            last_kernel, count,
            [spec(adj.shape, 1, b), spec(PACKED, 0), spec(PACKED, 0), spec(PACKED, 0, (first - start) // BLOCK)],
            spec(adj.shape, 1, b), f32(*adj.shape), "subtract", (adj, mid, mid_late, end), after, [out],
        )
        after = []
    return out[None]


def solution(mesh):
    return jax.shard_map(
        per_device,
        mesh=mesh,
        in_specs=(
            P("win", None, None, "tile", None),
            P("win", None, None, None, "tile", None),
            P("win", None, None, "tile", None),
        ),
        out_specs=P("win", None, None, "tile", None),
        check_vma=False,
    )
```

```python
import functools

import jax
import jax.numpy as jnp
from jax import lax
from jax.experimental import pallas as pl
from jax.experimental.pallas import tpu as pltpu
from jax.sharding import PartitionSpec as P

FIELDS, LON, LAT = 4, 16, 320
WIDE = 384
BLOCK = 4
FLOPS = (4000000000, 4000000000, 4000000000)
FIRST_VMEM = 54
MIB = 1024 * 1024
GROUPS = ((0, 24, False), (24, 8, True))
STEPS = ((1,), (0, 1))
ENDS = ((0, 24, 0), (24, 8, 1))


def wide(x):
    return jnp.concatenate([x, jnp.zeros((x.shape[0], WIDE - LAT), x.dtype)], axis=1)


def ends(x):
    row = lax.broadcasted_iota(jnp.int32, (8, x.shape[1]), 0)
    return jnp.where(row < 4, x[0:8], x[8:16])


def middle(x):
    row = lax.broadcasted_iota(jnp.int32, (8, x.shape[1]), 0)
    return jnp.where(row < 4, x[8:16], x[0:8])


def rates(a, b, c):
    along = a * (2.0 / 3.0)
    across = b * 0.5
    return dict(
        centre=1.0 - 4.0 * c,
        down=c + along,
        up=c - along,
        far=a * (1.0 / 12.0),
        lat_down=c + across,
        lat_up=c - across,
    )


def rolled(x, shift, axis):
    size = x.shape[axis]
    return pltpu.roll(x, shift % size, axis)


def inside(r, first, last):
    row = lax.broadcasted_iota(jnp.int32, r["far"].shape, 0)
    return dict(
        centre=r["centre"],
        lat_down=r["lat_down"],
        lat_up=r["lat_up"],
        down=jnp.where(row > first, r["down"], 0.0),
        up=jnp.where(row < last, r["up"], 0.0),
        far_down=jnp.where(row > first + 1, r["far"], 0.0),
        far_up=jnp.where(row < last - 1, r["far"], 0.0),
    )


def step(w, r):
    out = r["centre"] * w
    out += rolled(r["down"] * w, -1, 0) + rolled(r["up"] * w, 1, 0)
    out += rolled(r["far_up"] * w, 2, 0) - rolled(r["far_down"] * w, -2, 0)
    out += rolled(r["lat_down"] * w, -1, 1) + rolled(r["lat_up"] * w, 1, 1)
    return out


def leaving_rates(r):
    row = lax.broadcasted_iota(jnp.int32, r["far"].shape, 0)
    return dict(
        down=jnp.where(row == 0, r["down"], 0.0),
        up=jnp.where(row == 7, r["up"], 0.0),
        far_down=jnp.where(row < 2, r["far"], 0.0),
        far_up=jnp.where(row >= 6, r["far"], 0.0),
    )


def leaving(ws, r):
    to_next = 0.0
    to_previous = 0.0
    for f, w in enumerate(ws):
        to_next += rolled(r["up"] * w, 2 * f + 1, 0) + rolled(r["far_up"] * w, 2 * f + 2, 0)
        to_previous += rolled(r["down"] * w, 2 * f + 1, 0) - rolled(r["far_down"] * w, 2 * f, 0)
    return to_next, to_previous


def arriving(from_previous, from_next, f):
    row = lax.broadcasted_iota(jnp.int32, from_next.shape, 0)
    low = jnp.where(row < 2, rolled(from_previous, -2 * f, 0), 0.0)
    return jnp.where(row >= 6, rolled(from_next, 6 - 2 * f, 0), low)


def put_pair(ref, l, base, first, second):
    lane = lax.broadcasted_iota(jnp.int32, (8, 128), 1)
    ref[l, base : base + 8] = first[:, 0:128]
    ref[l, base + 8 : base + 16] = first[:, 128:256]
    ref[l, base + 16 : base + 24] = second[:, 0:128]
    ref[l, base + 24 : base + 32] = second[:, 128:256]
    ref[l, base + 32 : base + 40] = jnp.where(
        lane < 64, first[:, 256:384], pltpu.roll(second[:, 256:384], 64, 1)
    )


def put_packed(ref, l, pieces):
    for pair in range(FIELDS // 2):
        put_pair(ref, l, 40 * pair, pieces[2 * pair], pieces[2 * pair + 1])


def get_packed(ref, l, f, part):
    base = 40 * (f // 2)
    if part < 2:
        at = base + 16 * (f % 2) + 8 * part
        return ref[l, at : at + 8]
    last = ref[l, base + 32 : base + 40]
    return pltpu.roll(last, 64, 1) if f % 2 else last


def levels(body):
    pl.loop(0, BLOCK)(body)


def put_message(ref, l, now, then, r):
    put_pair(ref, l, 0, now, then)
    row = lax.broadcasted_iota(jnp.int32, (8, 128), 0)
    last = r[:, 256:384]
    rest = pltpu.roll(jnp.where(row < 2, last, 0.0), 6, 0)
    rest += pltpu.roll(pltpu.roll(jnp.where(row == 2, last, 0.0), 64, 1), 4, 0)
    ref[l, 40:48] = r[:, 0:128] + pltpu.roll(r[:, 128:256], 3, 0) + rest


def get_rate(message, k):
    last = message[46 + k % 2 : 47 + k % 2]
    if k == 2:
        last = pltpu.roll(jnp.broadcast_to(last, (8, 128)), 64, 1)
    parts = [message[40 + k : 41 + k], message[43 + k : 44 + k], last]
    return jnp.concatenate([jnp.broadcast_to(p, (8, 128)) for p in parts], axis=1)


def get_tile(message, k):
    base = 16 * k
    last = message[32:40]
    if k == 1:
        last = pltpu.roll(last, 64, 1)
    return jnp.concatenate([message[base : base + 8], message[base + 8 : base + 16], last], axis=1)


def leaving_rows(r):
    to_next = rolled(r["far_up"], 2, 0) + rolled(r["up"], 3, 0)
    to_previous = r["far_down"] + rolled(r["down"], 2, 0)
    return to_next, to_previous


def odd_tile():
    return lax.axis_index("tile") % 2 == 1


def first_kernel(base, blocks, adj, vel, kap, *refs):
    mid, image, partner, other, adj_buf, vel_buf, kap_buf, sem = refs[-8:]
    at = pl.program_id(0)

    def copies(block):
        rows = pl.ds(base + block * BLOCK, BLOCK)
        return [
            pltpu.make_async_copy(adj.at[:, rows], adj_buf.at[block], sem.at[block, 0]),
            pltpu.make_async_copy(vel.at[:, :, rows], vel_buf.at[block], sem.at[block, 1]),
            pltpu.make_async_copy(kap.at[:, rows], kap_buf.at[block], sem.at[block, 2]),
        ]

    @pl.when(at == 0)
    def _():
        for block in range(blocks):
            for copy in copies(block):
                copy.start()

    for copy in copies(at):
        copy.wait()
    adj, vel, kap = adj_buf.at[at], vel_buf.at[at], kap_buf.at[at]

    @levels
    def _(l):
        odd = odd_tile()
        ws = [wide(adj[f, l]) for f in range(FIELDS)]
        sent = []
        for s in (1, 0):
            r = rates(wide(vel[s, 0, l]), wide(vel[s, 1, l]), wide(kap[s, l]))
            out = leaving_rates({k: ends(v) for k, v in r.items() if k in ("down", "up", "far")})
            sent.append(leaving([ends(w) for w in ws], out))
            r = inside(r, 0, LON - 1)
            ws = [step(w, r) for w in ws]
        sent.append(leaving_rows(out))
        put_message(partner, l, *[jnp.where(odd, p, n) for n, p in sent])
        put_message(other, l, *[jnp.where(odd, n, p) for n, p in sent])
        put_packed(mid, l, [middle(w) for w in ws])
        for f, w in enumerate(ws):
            image[l, f] = ends(w)


def second_kernel(vel, kap, partner, other, from_partner, from_other, image, *refs):
    packed = refs[-1]

    @levels
    def _(l):
        odd = odd_tile()
        row = lax.broadcasted_iota(jnp.int32, (8, WIDE), 0)
        even_row = row % 2 == 0
        sides = []
        for (mine_even, mine_odd), (theirs_even, theirs_odd) in (
            ((other, partner), (from_other, from_partner)),
            ((partner, other), (from_partner, from_other)),
        ):
            mine = jnp.where(odd, mine_odd[l], mine_even[l])
            theirs = jnp.where(odd, theirs_odd[l], theirs_even[l])
            sides.append((get_tile(mine, 0), get_tile(theirs, 0), get_tile(theirs, 1), theirs))
        gave, low, low_then, theirs = sides[0]
        low_then += jnp.where(even_row, get_rate(theirs, 0), get_rate(theirs, 1)) * gave
        low_then += jnp.where(even_row, get_rate(theirs, 2) * rolled(gave, -1, 0), 0.0)
        gave, high, high_then, theirs = sides[1]
        high_then -= jnp.where(even_row, get_rate(theirs, 0), get_rate(theirs, 1)) * gave
        high_then += jnp.where(even_row, 0.0, get_rate(theirs, 2) * rolled(gave, 1, 0))
        r = rates(wide(ends(vel[0, 0, l])), wide(ends(vel[0, 1, l])), wide(ends(kap[0, l])))
        r = inside(r, 0, 7)
        pieces = []
        for f in range(FIELDS):
            new = arriving(low, high, f)
            pieces.append(image[l, f] + step(new, r) + arriving(low_then, high_then, f))
        put_packed(packed, l, pieces)


def last_kernel(direct, adj, end, mid, *refs):
    out = refs[-1]
    win, windows = lax.axis_index("win"), lax.axis_size("win")
    late, none = win == windows // 2 - 1, win == windows - 1
    mid_late = refs[0] if direct else None
    row = lax.broadcasted_iota(jnp.int32, (8, 128), 0)

    @levels
    def _(l):
        for f in range(FIELDS):
            for part in range(3):
                lanes = slice(128 * part, min(128 * part + 128, LAT))
                n = lanes.stop - lanes.start
                m, e = get_packed(mid, l, f, part), get_packed(end, l, f, part)
                if direct:
                    m = jnp.where(late, get_packed(mid_late, l, f, part), jnp.where(none, 0.0, m))
                out[f, l, 0:8, lanes] = adj[f, l, 0:8, lanes] - jnp.where(row < 4, e, m)[:, :n]
                out[f, l, 8:16, lanes] = adj[f, l, 8:16, lanes] - jnp.where(row < 4, m, e)[:, :n]


def spec(dims, at, first=0):
    block = tuple(BLOCK if i == at else d for i, d in enumerate(dims))
    return pl.BlockSpec(block, lambda i: tuple(first + i if k == at else 0 for k in range(len(dims))))


def f32(*dims):
    return jax.ShapeDtypeStruct(dims, jnp.float32)


def call(flops, kernel, count, in_specs, out_specs, out_shape, name, args, after=(), into=(), scratch=(), vmem=24):
    args, in_specs, aliases = list(args), list(in_specs), {}
    for extra in after:
        args.append(extra)
        in_specs.append(pl.BlockSpec(memory_space=pl.ANY))
    for k, buffer in enumerate(into):
        if buffer is not None:
            aliases[len(args)] = k
            args.append(buffer)
            in_specs.append(pl.BlockSpec(memory_space=pl.ANY))
    return pl.pallas_call(
        kernel,
        grid=(count // BLOCK,),
        in_specs=in_specs,
        out_specs=out_specs,
        out_shape=out_shape,
        scratch_shapes=list(scratch),
        name=name,
        input_output_aliases=aliases,
        cost_estimate=pl.CostEstimate(flops=flops, bytes_accessed=1, transcendentals=0),
        compiler_params=pltpu.CompilerParams(vmem_limit_bytes=vmem * MIB),
    )(*args)


MESSAGE = (0, 48, 128)
FIELD_TILES = (0, FIELDS, 8, WIDE)
PACKED = (0, 80, 128)


def sized(dims, n):
    return f32(n, *dims[1:])


def swapped(partner, other):
    n = lax.axis_size("tile")
    inner = [(i, i ^ 1) for i in range(n)]
    outer = [(i, (i + 1 if i % 2 else i - 1) % n) for i in range(n)]
    return lax.ppermute(partner, "tile", inner), lax.ppermute(other, "tile", outer)


def to_preceding(x):
    n = lax.axis_size("win")
    return lax.ppermute(x, "win", [(k + 1, k) for k in range(n - 1)])


def detour(x, step):
    n = lax.axis_size("win")
    if step:
        return lax.ppermute(x, "win", [(n - 1, n // 2 - 1)])
    return lax.ppermute(x, "win", [(k + 1, n - 1 if k + 1 == n // 2 else k) for k in range(n - 1)])


def long_way(x, step):
    n = lax.axis_size("win")
    h = n // 2
    side = ((h, h + 1), (h + 1, 2), (2, 3))[step]
    pairs = [(g + s, g + (s + 1) % h) for g in (0, h) for s in range(h) if s != step]
    return lax.ppermute(x, "win", [*pairs, side])


def per_device(adjoint, velocity, kappa):
    adj, vel, kap = adjoint[0], velocity[0], kappa[0]
    groups, after = [], []
    for start, n, around in GROUPS:
        blocks = n // BLOCK
        mid, image, *mine = call(
            FLOPS[0], functools.partial(first_kernel, start, blocks), n,
            [pl.BlockSpec(memory_space=pltpu.HBM)] * 3,
            [spec(d, 0) for d in (PACKED, FIELD_TILES, MESSAGE, MESSAGE)],
            [sized(d, n) for d in (PACKED, FIELD_TILES, MESSAGE, MESSAGE)],
            "interior", (adj, vel, kap), after, (),
            [
                pltpu.VMEM((blocks, FIELDS, BLOCK, LON, LAT), jnp.float32),
                pltpu.VMEM((blocks, 2, 2, BLOCK, LON, LAT), jnp.float32),
                pltpu.VMEM((blocks, 2, BLOCK, LON, LAT), jnp.float32),
                pltpu.SemaphoreType.DMA((blocks, 3)),
            ],
            FIRST_VMEM,
        )
        after = [mid]
        first_theirs = swapped(*mine) if not groups else None
        groups.append(([(long_way if around else detour)(mid, 0)], image, mine, first_theirs))
    lasts, after = [], []
    for k, (first, count, group) in enumerate(ENDS):
        start = GROUPS[group][0]
        mid, image, mine, ready = groups[group]
        if not lasts:
            theirs = ready
        elif group != ENDS[k - 1][2]:
            theirs = swapped(*mine)
            after = [*after, mid[0], groups[0][0][0]]
        b, c = first // BLOCK, (first - start) // BLOCK
        end = call(
            FLOPS[1], second_kernel, count,
            [spec((1, *vel.shape[1:]), 2, b), spec((1, *kap.shape[1:]), 1, b)]
            + [spec(d, 0, c) for d in (MESSAGE,) * 4 + (FIELD_TILES,)],
            spec(PACKED, 0), sized(PACKED, count), "ends", (vel, kap, *mine, *theirs, image), after,
        )
        after = [end]
        lasts.append(to_preceding(end))
        for at, (mid, _, _, _), (_, _, around) in zip(STEPS, groups, GROUPS):
            if k in at:
                x = lax.optimization_barrier([mid[-1], end])[0]
                mid.append((long_way if around else detour)(x, len(mid)))
    out, after = None, [end]
    for (first, count, group), end in zip(ENDS, lasts):
        b = first // BLOCK
        mid, around = groups[group][0], GROUPS[group][2]
        arrays = (adj, end, mid[-1]) if around else (adj, end, *mid)
        c = (first - GROUPS[group][0]) // BLOCK
        out = call(
            FLOPS[2], functools.partial(last_kernel, not around), count,
            [spec(adj.shape, 1, b), spec(PACKED, 0)] + [spec(PACKED, 0, c)] * (len(arrays) - 2),
            spec(adj.shape, 1, b), f32(*adj.shape), "subtract", arrays, after, [out],
        )
        after = []
    return out[None]


def solution(mesh):
    return jax.shard_map(
        per_device,
        mesh=mesh,
        in_specs=(
            P("win", None, None, "tile", None),
            P("win", None, None, None, "tile", None),
            P("win", None, None, "tile", None),
        ),
        out_specs=P("win", None, None, "tile", None),
        check_vma=False,
    )
```

```python
import functools

import jax
import jax.numpy as jnp
from jax import lax
from jax.experimental import pallas as pl
from jax.experimental.pallas import tpu as pltpu
from jax.sharding import PartitionSpec as P

FIELDS, LON, LAT = 4, 16, 320
WIDE = 384
BLOCK = 4
FLOPS = (8000000000, 8000000000, 8000000000)
FIRST_VMEM = 54
MIB = 1024 * 1024
GROUPS = ((0, 24, False), (24, 8, True))
SPLIT = 12
ENDS = ((0, 12, 0, 0), (12, 12, 0, 1), (24, 8, 1, 1))
STEPS = ((0,), (0, 2))


def wide(x):
    return jnp.concatenate([x, jnp.zeros((x.shape[0], WIDE - LAT), x.dtype)], axis=1)


def ends(x):
    row = lax.broadcasted_iota(jnp.int32, (8, x.shape[1]), 0)
    return jnp.where(row < 4, x[0:8], x[8:16])


def middle(x):
    row = lax.broadcasted_iota(jnp.int32, (8, x.shape[1]), 0)
    return jnp.where(row < 4, x[8:16], x[0:8])


def rates(a, b, c):
    along = a * (2.0 / 3.0)
    across = b * 0.5
    return dict(
        centre=1.0 - 4.0 * c,
        down=c + along,
        up=c - along,
        far=a * (1.0 / 12.0),
        lat_down=c + across,
        lat_up=c - across,
    )


def rolled(x, shift, axis):
    size = x.shape[axis]
    return pltpu.roll(x, shift % size, axis)


def inside(r, first, last):
    row = lax.broadcasted_iota(jnp.int32, r["far"].shape, 0)
    return dict(
        centre=r["centre"],
        lat_down=r["lat_down"],
        lat_up=r["lat_up"],
        down=jnp.where(row > first, r["down"], 0.0),
        up=jnp.where(row < last, r["up"], 0.0),
        far_down=jnp.where(row > first + 1, r["far"], 0.0),
        far_up=jnp.where(row < last - 1, r["far"], 0.0),
    )


def step(w, r):
    out = r["centre"] * w
    out += rolled(r["down"] * w, -1, 0) + rolled(r["up"] * w, 1, 0)
    out += rolled(r["far_up"] * w, 2, 0) - rolled(r["far_down"] * w, -2, 0)
    out += rolled(r["lat_down"] * w, -1, 1) + rolled(r["lat_up"] * w, 1, 1)
    return out


def leaving_rates(r):
    row = lax.broadcasted_iota(jnp.int32, r["far"].shape, 0)
    return dict(
        down=jnp.where(row == 0, r["down"], 0.0),
        up=jnp.where(row == 7, r["up"], 0.0),
        far_down=jnp.where(row < 2, r["far"], 0.0),
        far_up=jnp.where(row >= 6, r["far"], 0.0),
    )


def leaving(ws, r):
    to_next = 0.0
    to_previous = 0.0
    for f, w in enumerate(ws):
        to_next += rolled(r["up"] * w, 2 * f + 1, 0) + rolled(r["far_up"] * w, 2 * f + 2, 0)
        to_previous += rolled(r["down"] * w, 2 * f + 1, 0) - rolled(r["far_down"] * w, 2 * f, 0)
    return to_next, to_previous


def arriving(from_previous, from_next, f):
    row = lax.broadcasted_iota(jnp.int32, from_next.shape, 0)
    low = jnp.where(row < 2, rolled(from_previous, -2 * f, 0), 0.0)
    return jnp.where(row >= 6, rolled(from_next, 6 - 2 * f, 0), low)


def put_pair(ref, l, base, first, second):
    lane = lax.broadcasted_iota(jnp.int32, (8, 128), 1)
    ref[l, base : base + 8] = first[:, 0:128]
    ref[l, base + 8 : base + 16] = first[:, 128:256]
    ref[l, base + 16 : base + 24] = second[:, 0:128]
    ref[l, base + 24 : base + 32] = second[:, 128:256]
    ref[l, base + 32 : base + 40] = jnp.where(
        lane < 64, first[:, 256:384], pltpu.roll(second[:, 256:384], 64, 1)
    )


def put_packed(ref, l, pieces):
    for pair in range(FIELDS // 2):
        put_pair(ref, l, 40 * pair, pieces[2 * pair], pieces[2 * pair + 1])


def get_packed(ref, l, f, part):
    base = 40 * (f // 2)
    if part < 2:
        at = base + 16 * (f % 2) + 8 * part
        return ref[l, at : at + 8]
    last = ref[l, base + 32 : base + 40]
    return pltpu.roll(last, 64, 1) if f % 2 else last


def levels(body):
    pl.loop(0, BLOCK)(body)


def put_message(ref, l, now, then, r):
    put_pair(ref, l, 0, now, then)
    row = lax.broadcasted_iota(jnp.int32, (8, 128), 0)
    last = r[:, 256:384]
    rest = pltpu.roll(jnp.where(row < 2, last, 0.0), 6, 0)
    rest += pltpu.roll(pltpu.roll(jnp.where(row == 2, last, 0.0), 64, 1), 4, 0)
    ref[l, 40:48] = r[:, 0:128] + pltpu.roll(r[:, 128:256], 3, 0) + rest


def get_rate(message, k):
    last = message[46 + k % 2 : 47 + k % 2]
    if k == 2:
        last = pltpu.roll(jnp.broadcast_to(last, (8, 128)), 64, 1)
    parts = [message[40 + k : 41 + k], message[43 + k : 44 + k], last]
    return jnp.concatenate([jnp.broadcast_to(p, (8, 128)) for p in parts], axis=1)


def get_tile(message, k):
    base = 16 * k
    last = message[32:40]
    if k == 1:
        last = pltpu.roll(last, 64, 1)
    return jnp.concatenate([message[base : base + 8], message[base + 8 : base + 16], last], axis=1)


def leaving_rows(r):
    to_next = rolled(r["far_up"], 2, 0) + rolled(r["up"], 3, 0)
    to_previous = r["far_down"] + rolled(r["down"], 2, 0)
    return to_next, to_previous


def odd_tile():
    return lax.axis_index("tile") % 2 == 1


def first_kernel(base, blocks, outs, adj, vel, kap, *refs):
    adj_buf, vel_buf, kap_buf, sem = refs[-4:]
    mid, image, *messages = refs[-4 - outs : -4]
    at = pl.program_id(0)

    def copies(block):
        rows = pl.ds(base + block * BLOCK, BLOCK)
        return [
            pltpu.make_async_copy(adj.at[:, rows], adj_buf.at[block], sem.at[block, 0]),
            pltpu.make_async_copy(vel.at[:, :, rows], vel_buf.at[block], sem.at[block, 1]),
            pltpu.make_async_copy(kap.at[:, rows], kap_buf.at[block], sem.at[block, 2]),
        ]

    @pl.when(at == 0)
    def _():
        for block in range(blocks):
            for copy in copies(block):
                copy.start()

    for copy in copies(at):
        copy.wait()
    adj, vel, kap = adj_buf.at[at], vel_buf.at[at], kap_buf.at[at]

    def each(partner, other, l):
        odd = odd_tile()
        ws = [wide(adj[f, l]) for f in range(FIELDS)]
        sent = []
        for s in (1, 0):
            r = rates(wide(vel[s, 0, l]), wide(vel[s, 1, l]), wide(kap[s, l]))
            out = leaving_rates({k: ends(v) for k, v in r.items() if k in ("down", "up", "far")})
            sent.append(leaving([ends(w) for w in ws], out))
            r = inside(r, 0, LON - 1)
            ws = [step(w, r) for w in ws]
        sent.append(leaving_rows(out))
        put_message(partner, l, *[jnp.where(odd, p, n) for n, p in sent])
        put_message(other, l, *[jnp.where(odd, n, p) for n, p in sent])
        put_packed(mid, l, [middle(w) for w in ws])
        for f, w in enumerate(ws):
            image[l, f] = ends(w)

    if len(messages) == 2:
        levels(functools.partial(each, *messages))
    else:

        @pl.when(at < SPLIT // BLOCK)
        def _():
            levels(functools.partial(each, *messages[:2]))

        @pl.when(at >= SPLIT // BLOCK)
        def _():
            levels(functools.partial(each, *messages[2:]))


def second_kernel(vel, kap, partner, other, from_partner, from_other, image, *refs):
    packed = refs[-1]

    @levels
    def _(l):
        odd = odd_tile()
        row = lax.broadcasted_iota(jnp.int32, (8, WIDE), 0)
        even_row = row % 2 == 0
        sides = []
        for (mine_even, mine_odd), (theirs_even, theirs_odd) in (
            ((other, partner), (from_other, from_partner)),
            ((partner, other), (from_partner, from_other)),
        ):
            mine = jnp.where(odd, mine_odd[l], mine_even[l])
            theirs = jnp.where(odd, theirs_odd[l], theirs_even[l])
            sides.append((get_tile(mine, 0), get_tile(theirs, 0), get_tile(theirs, 1), theirs))
        gave, low, low_then, theirs = sides[0]
        low_then += jnp.where(even_row, get_rate(theirs, 0), get_rate(theirs, 1)) * gave
        low_then += jnp.where(even_row, get_rate(theirs, 2) * rolled(gave, -1, 0), 0.0)
        gave, high, high_then, theirs = sides[1]
        high_then -= jnp.where(even_row, get_rate(theirs, 0), get_rate(theirs, 1)) * gave
        high_then += jnp.where(even_row, 0.0, get_rate(theirs, 2) * rolled(gave, 1, 0))
        r = rates(wide(ends(vel[0, 0, l])), wide(ends(vel[0, 1, l])), wide(ends(kap[0, l])))
        r = inside(r, 0, 7)
        pieces = []
        for f in range(FIELDS):
            new = arriving(low, high, f)
            pieces.append(image[l, f] + step(new, r) + arriving(low_then, high_then, f))
        put_packed(packed, l, pieces)


def last_kernel(direct, adj, end, mid, *refs):
    out = refs[-1]
    win, windows = lax.axis_index("win"), lax.axis_size("win")
    late, none = win == windows // 2 - 1, win == windows - 1
    mid_late = refs[0] if direct else None
    row = lax.broadcasted_iota(jnp.int32, (8, 128), 0)

    @levels
    def _(l):
        for f in range(FIELDS):
            for part in range(3):
                lanes = slice(128 * part, min(128 * part + 128, LAT))
                n = lanes.stop - lanes.start
                m, e = get_packed(mid, l, f, part), get_packed(end, l, f, part)
                if direct:
                    m = jnp.where(late, get_packed(mid_late, l, f, part), jnp.where(none, 0.0, m))
                out[f, l, 0:8, lanes] = adj[f, l, 0:8, lanes] - jnp.where(row < 4, e, m)[:, :n]
                out[f, l, 8:16, lanes] = adj[f, l, 8:16, lanes] - jnp.where(row < 4, m, e)[:, :n]


def spec(dims, at, first=0):
    block = tuple(BLOCK if i == at else d for i, d in enumerate(dims))
    return pl.BlockSpec(block, lambda i: tuple(first + i if k == at else 0 for k in range(len(dims))))


def part_spec(begin, end):
    return pl.BlockSpec((BLOCK, *MESSAGE[1:]), lambda i: (jnp.clip(i - begin, 0, end - begin - 1), 0, 0))


def f32(*dims):
    return jax.ShapeDtypeStruct(dims, jnp.float32)


def call(flops, kernel, count, in_specs, out_specs, out_shape, name, args, after=(), into=(), scratch=(), vmem=24):
    args, in_specs, aliases = list(args), list(in_specs), {}
    for extra in after:
        args.append(extra)
        in_specs.append(pl.BlockSpec(memory_space=pl.ANY))
    for k, buffer in enumerate(into):
        if buffer is not None:
            aliases[len(args)] = k
            args.append(buffer)
            in_specs.append(pl.BlockSpec(memory_space=pl.ANY))
    return pl.pallas_call(
        kernel,
        grid=(count // BLOCK,),
        in_specs=in_specs,
        out_specs=out_specs,
        out_shape=out_shape,
        scratch_shapes=list(scratch),
        name=name,
        input_output_aliases=aliases,
        cost_estimate=pl.CostEstimate(flops=flops, bytes_accessed=1, transcendentals=0),
        compiler_params=pltpu.CompilerParams(vmem_limit_bytes=vmem * MIB),
    )(*args)


MESSAGE = (0, 48, 128)
FIELD_TILES = (0, FIELDS, 8, WIDE)
PACKED = (0, 80, 128)


def sized(dims, n):
    return f32(n, *dims[1:])


def swapped(partner, other):
    n = lax.axis_size("tile")
    inner = [(i, i ^ 1) for i in range(n)]
    outer = [(i, (i + 1 if i % 2 else i - 1) % n) for i in range(n)]
    return lax.ppermute(partner, "tile", inner), lax.ppermute(other, "tile", outer)


def to_preceding(x):
    n = lax.axis_size("win")
    return lax.ppermute(x, "win", [(k + 1, k) for k in range(n - 1)])


def detour(x, step):
    n = lax.axis_size("win")
    if step:
        return lax.ppermute(x, "win", [(n - 1, n // 2 - 1)])
    return lax.ppermute(x, "win", [(k + 1, n - 1 if k + 1 == n // 2 else k) for k in range(n - 1)])


def long_way(x, step):
    n = lax.axis_size("win")
    h = n // 2
    side = ((h, h + 1), (h + 1, 2), (2, 3))[step]
    pairs = [(g + s, g + (s + 1) % h) for g in (0, h) for s in range(h) if s != step]
    return lax.ppermute(x, "win", [*pairs, side])


def per_device(adjoint, velocity, kappa):
    adj, vel, kap = adjoint[0], velocity[0], kappa[0]
    scratch = [
        (FIELDS, BLOCK, LON, LAT),
        (2, 2, BLOCK, LON, LAT),
        (2, BLOCK, LON, LAT),
    ]
    groups, after = [], []
    cut, rest = SPLIT // BLOCK, sized(MESSAGE, sum(n for _, n, _ in GROUPS) - SPLIT)
    early = late = None
    for start, n, around in GROUPS:
        blocks = n // BLOCK
        if early is None:
            specs = [part_spec(0, cut)] * 2 + [part_spec(cut, blocks)] * 2
            shapes, into = [sized(MESSAGE, SPLIT)] * 2 + [rest] * 2, ()
        else:
            specs = [spec(MESSAGE, 0, (start - SPLIT) // BLOCK)] * 2
            shapes, into = [rest] * 2, (None, None, *late)
        mid, image, *mine = call(
            FLOPS[0], functools.partial(first_kernel, start, blocks, 2 + len(specs)), n,
            [pl.BlockSpec(memory_space=pltpu.HBM)] * 3,
            [spec(d, 0) for d in (PACKED, FIELD_TILES)] + specs,
            [sized(d, n) for d in (PACKED, FIELD_TILES)] + shapes,
            "interior", (adj, vel, kap), after, into,
            [pltpu.VMEM((blocks, *d), jnp.float32) for d in scratch] + [pltpu.SemaphoreType.DMA((blocks, 3))],
            FIRST_VMEM,
        )
        after = [mid]
        if early is None:
            early = mine[:2]
            early_theirs = swapped(*early)
        late = mine[-2:]
        groups.append(([(long_way if around else detour)(mid, 0)], image))
    exchanges = ((early, early_theirs), (late, swapped(*late)))
    lasts, after = [], []
    for k, (first, count, group, exchange) in enumerate(ENDS):
        mine, theirs = exchanges[exchange]
        b = first // BLOCK
        c, m = (first - GROUPS[group][0]) // BLOCK, (first - SPLIT * exchange) // BLOCK
        if k == 1:
            after = [*after, groups[1][0][0]]
        end = call(
            FLOPS[1], second_kernel, count,
            [spec((1, *vel.shape[1:]), 2, b), spec((1, *kap.shape[1:]), 1, b)]
            + [spec(MESSAGE, 0, m)] * 4 + [spec(FIELD_TILES, 0, c)],
            spec(PACKED, 0), sized(PACKED, count), "ends", (vel, kap, *mine, *theirs, groups[group][1]), after,
        )
        after = [end]
        lasts.append(to_preceding(end))
        for at, (mid, _), (_, _, around) in zip(STEPS, groups, GROUPS):
            if k in at:
                x = lax.optimization_barrier([mid[-1], end])[0]
                mid.append((long_way if around else detour)(x, len(mid)))
    out, after = None, [end]
    for (first, count, group, _), end in zip(ENDS, lasts):
        b = first // BLOCK
        mid, around = groups[group][0], GROUPS[group][2]
        arrays = (adj, end, mid[-1]) if around else (adj, end, *mid)
        c = (first - GROUPS[group][0]) // BLOCK
        out = call(
            FLOPS[2], functools.partial(last_kernel, not around), count,
            [spec(adj.shape, 1, b), spec(PACKED, 0)] + [spec(PACKED, 0, c)] * (len(arrays) - 2),
            spec(adj.shape, 1, b), f32(*adj.shape), "subtract", arrays, after, [out],
        )
        after = []
    return out[None]


def solution(mesh):
    return jax.shard_map(
        per_device,
        mesh=mesh,
        in_specs=(
            P("win", None, None, "tile", None),
            P("win", None, None, None, "tile", None),
            P("win", None, None, "tile", None),
        ),
        out_specs=P("win", None, None, "tile", None),
        check_vma=False,
    )
```

```python
import functools

import jax
import jax.numpy as jnp
from jax import lax
from jax.experimental import pallas as pl
from jax.experimental.pallas import tpu as pltpu
from jax.sharding import PartitionSpec as P

FIELDS, LON, LAT = 4, 16, 320
WIDE = 384
BLOCK = 4
FLOPS = (4000000000, 6000000000, 4000000000)
FIRST_VMEM = 54
MIB = 1024 * 1024
GROUPS = ((0, 24, False), (24, 8, True))
SPLIT = 12
ENDS = ((0, 12, 0, 0), (12, 12, 0, 1), (24, 8, 1, 1))
STEPS = ((0,), (0, 2))


def wide(x):
    return jnp.concatenate([x, jnp.zeros((x.shape[0], WIDE - LAT), x.dtype)], axis=1)


def ends(x):
    row = lax.broadcasted_iota(jnp.int32, (8, x.shape[1]), 0)
    return jnp.where(row < 4, x[0:8], x[8:16])


def middle(x):
    row = lax.broadcasted_iota(jnp.int32, (8, x.shape[1]), 0)
    return jnp.where(row < 4, x[8:16], x[0:8])


def rates(a, b, c):
    along = a * (2.0 / 3.0)
    across = b * 0.5
    return dict(
        centre=1.0 - 4.0 * c,
        down=c + along,
        up=c - along,
        far=a * (1.0 / 12.0),
        lat_down=c + across,
        lat_up=c - across,
    )


def rolled(x, shift, axis):
    size = x.shape[axis]
    return pltpu.roll(x, shift % size, axis)


def inside(r, first, last):
    row = lax.broadcasted_iota(jnp.int32, r["far"].shape, 0)
    return dict(
        centre=r["centre"],
        lat_down=r["lat_down"],
        lat_up=r["lat_up"],
        down=jnp.where(row > first, r["down"], 0.0),
        up=jnp.where(row < last, r["up"], 0.0),
        far_down=jnp.where(row > first + 1, r["far"], 0.0),
        far_up=jnp.where(row < last - 1, r["far"], 0.0),
    )


def step(w, r):
    out = r["centre"] * w
    out += rolled(r["down"] * w, -1, 0) + rolled(r["up"] * w, 1, 0)
    out += rolled(r["far_up"] * w, 2, 0) - rolled(r["far_down"] * w, -2, 0)
    out += rolled(r["lat_down"] * w, -1, 1) + rolled(r["lat_up"] * w, 1, 1)
    return out


def leaving_rates(r):
    row = lax.broadcasted_iota(jnp.int32, r["far"].shape, 0)
    return dict(
        down=jnp.where(row == 0, r["down"], 0.0),
        up=jnp.where(row == 7, r["up"], 0.0),
        far_down=jnp.where(row < 2, r["far"], 0.0),
        far_up=jnp.where(row >= 6, r["far"], 0.0),
    )


def leaving(ws, r):
    to_next = 0.0
    to_previous = 0.0
    for f, w in enumerate(ws):
        to_next += rolled(r["up"] * w, 2 * f + 1, 0) + rolled(r["far_up"] * w, 2 * f + 2, 0)
        to_previous += rolled(r["down"] * w, 2 * f + 1, 0) - rolled(r["far_down"] * w, 2 * f, 0)
    return to_next, to_previous


def arriving(from_previous, from_next, f):
    row = lax.broadcasted_iota(jnp.int32, from_next.shape, 0)
    low = jnp.where(row < 2, rolled(from_previous, -2 * f, 0), 0.0)
    return jnp.where(row >= 6, rolled(from_next, 6 - 2 * f, 0), low)


def put_pair(ref, l, base, first, second):
    lane = lax.broadcasted_iota(jnp.int32, (8, 128), 1)
    ref[l, base : base + 8] = first[:, 0:128]
    ref[l, base + 8 : base + 16] = first[:, 128:256]
    ref[l, base + 16 : base + 24] = second[:, 0:128]
    ref[l, base + 24 : base + 32] = second[:, 128:256]
    ref[l, base + 32 : base + 40] = jnp.where(
        lane < 64, first[:, 256:384], pltpu.roll(second[:, 256:384], 64, 1)
    )


def put_packed(ref, l, pieces):
    for pair in range(FIELDS // 2):
        put_pair(ref, l, 40 * pair, pieces[2 * pair], pieces[2 * pair + 1])


def get_packed(ref, l, f, part):
    base = 40 * (f // 2)
    if part < 2:
        at = base + 16 * (f % 2) + 8 * part
        return ref[l, at : at + 8]
    last = ref[l, base + 32 : base + 40]
    return pltpu.roll(last, 64, 1) if f % 2 else last


def levels(body):
    pl.loop(0, BLOCK)(body)


def put_message(ref, l, now, then, r):
    put_pair(ref, l, 0, now, then)
    row = lax.broadcasted_iota(jnp.int32, (8, 128), 0)
    last = r[:, 256:384]
    rest = pltpu.roll(jnp.where(row < 2, last, 0.0), 6, 0)
    rest += pltpu.roll(pltpu.roll(jnp.where(row == 2, last, 0.0), 64, 1), 4, 0)
    ref[l, 40:48] = r[:, 0:128] + pltpu.roll(r[:, 128:256], 3, 0) + rest


def get_rate(message, k):
    last = message[46 + k % 2 : 47 + k % 2]
    if k == 2:
        last = pltpu.roll(jnp.broadcast_to(last, (8, 128)), 64, 1)
    parts = [message[40 + k : 41 + k], message[43 + k : 44 + k], last]
    return jnp.concatenate([jnp.broadcast_to(p, (8, 128)) for p in parts], axis=1)


def get_tile(message, k):
    base = 16 * k
    last = message[32:40]
    if k == 1:
        last = pltpu.roll(last, 64, 1)
    return jnp.concatenate([message[base : base + 8], message[base + 8 : base + 16], last], axis=1)


def leaving_rows(r):
    to_next = rolled(r["far_up"], 2, 0) + rolled(r["up"], 3, 0)
    to_previous = r["far_down"] + rolled(r["down"], 2, 0)
    return to_next, to_previous


def odd_tile():
    return lax.axis_index("tile") % 2 == 1


def first_kernel(base, blocks, outs, adj, vel, kap, *refs):
    adj_buf, vel_buf, kap_buf, sem = refs[-4:]
    mid, image, *messages = refs[-4 - outs : -4]
    at = pl.program_id(0)

    def copies(block):
        rows = pl.ds(base + block * BLOCK, BLOCK)
        return [
            pltpu.make_async_copy(adj.at[:, rows], adj_buf.at[block], sem.at[block, 0]),
            pltpu.make_async_copy(vel.at[:, :, rows], vel_buf.at[block], sem.at[block, 1]),
            pltpu.make_async_copy(kap.at[:, rows], kap_buf.at[block], sem.at[block, 2]),
        ]

    @pl.when(at == 0)
    def _():
        for block in range(blocks):
            for copy in copies(block):
                copy.start()

    for copy in copies(at):
        copy.wait()
    adj, vel, kap = adj_buf.at[at], vel_buf.at[at], kap_buf.at[at]

    def each(partner, other, l):
        odd = odd_tile()
        ws = [wide(adj[f, l]) for f in range(FIELDS)]
        sent = []
        for s in (1, 0):
            r = rates(wide(vel[s, 0, l]), wide(vel[s, 1, l]), wide(kap[s, l]))
            out = leaving_rates({k: ends(v) for k, v in r.items() if k in ("down", "up", "far")})
            sent.append(leaving([ends(w) for w in ws], out))
            r = inside(r, 0, LON - 1)
            ws = [step(w, r) for w in ws]
        sent.append(leaving_rows(out))
        put_message(partner, l, *[jnp.where(odd, p, n) for n, p in sent])
        put_message(other, l, *[jnp.where(odd, n, p) for n, p in sent])
        put_packed(mid, l, [middle(w) for w in ws])
        for f, w in enumerate(ws):
            image[l, f] = ends(w)

    if len(messages) == 2:
        levels(functools.partial(each, *messages))
    else:

        @pl.when(at < SPLIT // BLOCK)
        def _():
            levels(functools.partial(each, *messages[:2]))

        @pl.when(at >= SPLIT // BLOCK)
        def _():
            levels(functools.partial(each, *messages[2:]))


def second_kernel(vel, kap, partner, other, from_partner, from_other, image, *refs):
    packed = refs[-1]

    @levels
    def _(l):
        odd = odd_tile()
        row = lax.broadcasted_iota(jnp.int32, (8, WIDE), 0)
        even_row = row % 2 == 0
        sides = []
        for (mine_even, mine_odd), (theirs_even, theirs_odd) in (
            ((other, partner), (from_other, from_partner)),
            ((partner, other), (from_partner, from_other)),
        ):
            mine = jnp.where(odd, mine_odd[l], mine_even[l])
            theirs = jnp.where(odd, theirs_odd[l], theirs_even[l])
            sides.append((get_tile(mine, 0), get_tile(theirs, 0), get_tile(theirs, 1), theirs))
        gave, low, low_then, theirs = sides[0]
        low_then += jnp.where(even_row, get_rate(theirs, 0), get_rate(theirs, 1)) * gave
        low_then += jnp.where(even_row, get_rate(theirs, 2) * rolled(gave, -1, 0), 0.0)
        gave, high, high_then, theirs = sides[1]
        high_then -= jnp.where(even_row, get_rate(theirs, 0), get_rate(theirs, 1)) * gave
        high_then += jnp.where(even_row, 0.0, get_rate(theirs, 2) * rolled(gave, 1, 0))
        r = rates(wide(ends(vel[0, 0, l])), wide(ends(vel[0, 1, l])), wide(ends(kap[0, l])))
        r = inside(r, 0, 7)
        pieces = []
        for f in range(FIELDS):
            new = arriving(low, high, f)
            pieces.append(image[l, f] + step(new, r) + arriving(low_then, high_then, f))
        put_packed(packed, l, pieces)


def last_kernel(direct, adj, end, mid, *refs):
    out = refs[-1]
    win, windows = lax.axis_index("win"), lax.axis_size("win")
    late, none = win == windows // 2 - 1, win == windows - 1
    mid_late = refs[0] if direct else None
    row = lax.broadcasted_iota(jnp.int32, (8, 128), 0)

    @levels
    def _(l):
        for f in range(FIELDS):
            for part in range(3):
                lanes = slice(128 * part, min(128 * part + 128, LAT))
                n = lanes.stop - lanes.start
                m, e = get_packed(mid, l, f, part), get_packed(end, l, f, part)
                if direct:
                    m = jnp.where(late, get_packed(mid_late, l, f, part), jnp.where(none, 0.0, m))
                out[f, l, 0:8, lanes] = adj[f, l, 0:8, lanes] - jnp.where(row < 4, e, m)[:, :n]
                out[f, l, 8:16, lanes] = adj[f, l, 8:16, lanes] - jnp.where(row < 4, m, e)[:, :n]


def spec(dims, at, first=0):
    block = tuple(BLOCK if i == at else d for i, d in enumerate(dims))
    return pl.BlockSpec(block, lambda i: tuple(first + i if k == at else 0 for k in range(len(dims))))


def part_spec(begin, end):
    return pl.BlockSpec((BLOCK, *MESSAGE[1:]), lambda i: (jnp.clip(i - begin, 0, end - begin - 1), 0, 0))


def f32(*dims):
    return jax.ShapeDtypeStruct(dims, jnp.float32)


def call(flops, kernel, count, in_specs, out_specs, out_shape, name, args, after=(), into=(), scratch=(), vmem=24):
    args, in_specs, aliases = list(args), list(in_specs), {}
    for extra in after:
        args.append(extra)
        in_specs.append(pl.BlockSpec(memory_space=pl.ANY))
    for k, buffer in enumerate(into):
        if buffer is not None:
            aliases[len(args)] = k
            args.append(buffer)
            in_specs.append(pl.BlockSpec(memory_space=pl.ANY))
    return pl.pallas_call(
        kernel,
        grid=(count // BLOCK,),
        in_specs=in_specs,
        out_specs=out_specs,
        out_shape=out_shape,
        scratch_shapes=list(scratch),
        name=name,
        input_output_aliases=aliases,
        cost_estimate=pl.CostEstimate(flops=flops, bytes_accessed=1, transcendentals=0),
        compiler_params=pltpu.CompilerParams(vmem_limit_bytes=vmem * MIB),
    )(*args)


MESSAGE = (0, 48, 128)
FIELD_TILES = (0, FIELDS, 8, WIDE)
PACKED = (0, 80, 128)


def sized(dims, n):
    return f32(n, *dims[1:])


def swapped(partner, other):
    n = lax.axis_size("tile")
    inner = [(i, i ^ 1) for i in range(n)]
    outer = [(i, (i + 1 if i % 2 else i - 1) % n) for i in range(n)]
    return lax.ppermute(partner, "tile", inner), lax.ppermute(other, "tile", outer)


def to_preceding(x):
    n = lax.axis_size("win")
    return lax.ppermute(x, "win", [(k + 1, k) for k in range(n - 1)])


def detour(x, step):
    n = lax.axis_size("win")
    if step:
        return lax.ppermute(x, "win", [(n - 1, n // 2 - 1)])
    return lax.ppermute(x, "win", [(k + 1, n - 1 if k + 1 == n // 2 else k) for k in range(n - 1)])


def long_way(x, step):
    n = lax.axis_size("win")
    h = n // 2
    side = ((h, h + 1), (h + 1, 2), (2, 3))[step]
    pairs = [(g + s, g + (s + 1) % h) for g in (0, h) for s in range(h) if s != step]
    return lax.ppermute(x, "win", [*pairs, side])


def per_device(adjoint, velocity, kappa):
    adj, vel, kap = adjoint[0], velocity[0], kappa[0]
    scratch = [
        (FIELDS, BLOCK, LON, LAT),
        (2, 2, BLOCK, LON, LAT),
        (2, BLOCK, LON, LAT),
    ]
    groups, after = [], []
    cut, rest = SPLIT // BLOCK, sized(MESSAGE, sum(n for _, n, _ in GROUPS) - SPLIT)
    early = late = None
    for start, n, around in GROUPS:
        blocks = n // BLOCK
        if early is None:
            specs = [part_spec(0, cut)] * 2 + [part_spec(cut, blocks)] * 2
            shapes, into = [sized(MESSAGE, SPLIT)] * 2 + [rest] * 2, ()
        else:
            specs = [spec(MESSAGE, 0, (start - SPLIT) // BLOCK)] * 2
            shapes, into = [rest] * 2, (None, None, *late)
        mid, image, *mine = call(
            FLOPS[0], functools.partial(first_kernel, start, blocks, 2 + len(specs)), n,
            [pl.BlockSpec(memory_space=pltpu.HBM)] * 3,
            [spec(d, 0) for d in (PACKED, FIELD_TILES)] + specs,
            [sized(d, n) for d in (PACKED, FIELD_TILES)] + shapes,
            "interior", (adj, vel, kap), after, into,
            [pltpu.VMEM((blocks, *d), jnp.float32) for d in scratch] + [pltpu.SemaphoreType.DMA((blocks, 3))],
            FIRST_VMEM,
        )
        after = [mid]
        if early is None:
            early = mine[:2]
            early_theirs = swapped(*early)
        late = mine[-2:]
        groups.append(([(long_way if around else detour)(mid, 0)], image))
    exchanges = ((early, early_theirs), (late, swapped(*late)))
    lasts, after = [], []
    for k, (first, count, group, exchange) in enumerate(ENDS):
        mine, theirs = exchanges[exchange]
        b = first // BLOCK
        c, m = (first - GROUPS[group][0]) // BLOCK, (first - SPLIT * exchange) // BLOCK
        if k == 1:
            after = [*after, groups[1][0][0]]
        end = call(
            FLOPS[1], second_kernel, count,
            [spec((1, *vel.shape[1:]), 2, b), spec((1, *kap.shape[1:]), 1, b)]
            + [spec(MESSAGE, 0, m)] * 4 + [spec(FIELD_TILES, 0, c)],
            spec(PACKED, 0), sized(PACKED, count), "ends", (vel, kap, *mine, *theirs, groups[group][1]), after,
        )
        after = [end]
        lasts.append(to_preceding(end))
        for at, (mid, _), (_, _, around) in zip(STEPS, groups, GROUPS):
            if k in at:
                x = lax.optimization_barrier([mid[-1], end])[0]
                mid.append((long_way if around else detour)(x, len(mid)))
    out, after = None, [end]
    for (first, count, group, _), end in zip(ENDS, lasts):
        b = first // BLOCK
        mid, around = groups[group][0], GROUPS[group][2]
        arrays = (adj, end, mid[-1]) if around else (adj, end, *mid)
        c = (first - GROUPS[group][0]) // BLOCK
        out = call(
            FLOPS[2], functools.partial(last_kernel, not around), count,
            [spec(adj.shape, 1, b), spec(PACKED, 0)] + [spec(PACKED, 0, c)] * (len(arrays) - 2),
            spec(adj.shape, 1, b), f32(*adj.shape), "subtract", arrays, after, [out],
        )
        after = []
    return out[None]


def solution(mesh):
    return jax.shard_map(
        per_device,
        mesh=mesh,
        in_specs=(
            P("win", None, None, "tile", None),
            P("win", None, None, None, "tile", None),
            P("win", None, None, "tile", None),
        ),
        out_specs=P("win", None, None, "tile", None),
        check_vma=False,
    )
```

```python
import functools

import jax
import jax.numpy as jnp
from jax import lax
from jax.experimental import pallas as pl
from jax.experimental.pallas import tpu as pltpu
from jax.sharding import PartitionSpec as P

FIELDS, LON, LAT = 4, 16, 320
WIDE = 384
BLOCK = 4
FLOPS = (8000000000, 8000000000, 8000000000)
FIRST_VMEM = 54
MIB = 1024 * 1024
GROUPS = ((0, 24, False), (24, 8, True))
SPLIT = 16
ENDS = ((0, 16, 0, 0), (16, 8, 0, 1), (24, 8, 1, 1))
STEPS = ((0,), (0, 2))


def wide(x):
    return jnp.concatenate([x, jnp.zeros((x.shape[0], WIDE - LAT), x.dtype)], axis=1)


def ends(x):
    row = lax.broadcasted_iota(jnp.int32, (8, x.shape[1]), 0)
    return jnp.where(row < 4, x[0:8], x[8:16])


def middle(x):
    row = lax.broadcasted_iota(jnp.int32, (8, x.shape[1]), 0)
    return jnp.where(row < 4, x[8:16], x[0:8])


def rates(a, b, c):
    along = a * (2.0 / 3.0)
    across = b * 0.5
    return dict(
        centre=1.0 - 4.0 * c,
        down=c + along,
        up=c - along,
        far=a * (1.0 / 12.0),
        lat_down=c + across,
        lat_up=c - across,
    )


def rolled(x, shift, axis):
    size = x.shape[axis]
    return pltpu.roll(x, shift % size, axis)


def inside(r, first, last):
    row = lax.broadcasted_iota(jnp.int32, r["far"].shape, 0)
    return dict(
        centre=r["centre"],
        lat_down=r["lat_down"],
        lat_up=r["lat_up"],
        down=jnp.where(row > first, r["down"], 0.0),
        up=jnp.where(row < last, r["up"], 0.0),
        far_down=jnp.where(row > first + 1, r["far"], 0.0),
        far_up=jnp.where(row < last - 1, r["far"], 0.0),
    )


def step(w, r):
    out = r["centre"] * w
    out += rolled(r["down"] * w, -1, 0) + rolled(r["up"] * w, 1, 0)
    out += rolled(r["far_up"] * w, 2, 0) - rolled(r["far_down"] * w, -2, 0)
    out += rolled(r["lat_down"] * w, -1, 1) + rolled(r["lat_up"] * w, 1, 1)
    return out


def leaving_rates(r):
    row = lax.broadcasted_iota(jnp.int32, r["far"].shape, 0)
    return dict(
        down=jnp.where(row == 0, r["down"], 0.0),
        up=jnp.where(row == 7, r["up"], 0.0),
        far_down=jnp.where(row < 2, r["far"], 0.0),
        far_up=jnp.where(row >= 6, r["far"], 0.0),
    )


def leaving(ws, r):
    to_next = 0.0
    to_previous = 0.0
    for f, w in enumerate(ws):
        to_next += rolled(r["up"] * w, 2 * f + 1, 0) + rolled(r["far_up"] * w, 2 * f + 2, 0)
        to_previous += rolled(r["down"] * w, 2 * f + 1, 0) - rolled(r["far_down"] * w, 2 * f, 0)
    return to_next, to_previous


def arriving(from_previous, from_next, f):
    row = lax.broadcasted_iota(jnp.int32, from_next.shape, 0)
    low = jnp.where(row < 2, rolled(from_previous, -2 * f, 0), 0.0)
    return jnp.where(row >= 6, rolled(from_next, 6 - 2 * f, 0), low)


def put_pair(ref, l, base, first, second):
    lane = lax.broadcasted_iota(jnp.int32, (8, 128), 1)
    ref[l, base : base + 8] = first[:, 0:128]
    ref[l, base + 8 : base + 16] = first[:, 128:256]
    ref[l, base + 16 : base + 24] = second[:, 0:128]
    ref[l, base + 24 : base + 32] = second[:, 128:256]
    ref[l, base + 32 : base + 40] = jnp.where(
        lane < 64, first[:, 256:384], pltpu.roll(second[:, 256:384], 64, 1)
    )


def put_packed(ref, l, pieces):
    for pair in range(FIELDS // 2):
        put_pair(ref, l, 40 * pair, pieces[2 * pair], pieces[2 * pair + 1])


def get_packed(ref, l, f, part):
    base = 40 * (f // 2)
    if part < 2:
        at = base + 16 * (f % 2) + 8 * part
        return ref[l, at : at + 8]
    last = ref[l, base + 32 : base + 40]
    return pltpu.roll(last, 64, 1) if f % 2 else last


def levels(body):
    pl.loop(0, BLOCK)(body)


def put_message(ref, l, now, then, r):
    put_pair(ref, l, 0, now, then)
    row = lax.broadcasted_iota(jnp.int32, (8, 128), 0)
    last = r[:, 256:384]
    rest = pltpu.roll(jnp.where(row < 2, last, 0.0), 6, 0)
    rest += pltpu.roll(pltpu.roll(jnp.where(row == 2, last, 0.0), 64, 1), 4, 0)
    ref[l, 40:48] = r[:, 0:128] + pltpu.roll(r[:, 128:256], 3, 0) + rest


def get_rate(message, k):
    last = message[46 + k % 2 : 47 + k % 2]
    if k == 2:
        last = pltpu.roll(jnp.broadcast_to(last, (8, 128)), 64, 1)
    parts = [message[40 + k : 41 + k], message[43 + k : 44 + k], last]
    return jnp.concatenate([jnp.broadcast_to(p, (8, 128)) for p in parts], axis=1)


def get_tile(message, k):
    base = 16 * k
    last = message[32:40]
    if k == 1:
        last = pltpu.roll(last, 64, 1)
    return jnp.concatenate([message[base : base + 8], message[base + 8 : base + 16], last], axis=1)


def leaving_rows(r):
    to_next = rolled(r["far_up"], 2, 0) + rolled(r["up"], 3, 0)
    to_previous = r["far_down"] + rolled(r["down"], 2, 0)
    return to_next, to_previous


def odd_tile():
    return lax.axis_index("tile") % 2 == 1


def first_kernel(base, blocks, outs, adj, vel, kap, *refs):
    adj_buf, vel_buf, kap_buf, sem = refs[-4:]
    mid, image, *messages = refs[-4 - outs : -4]
    at = pl.program_id(0)

    def copies(block):
        rows = pl.ds(base + block * BLOCK, BLOCK)
        return [
            pltpu.make_async_copy(adj.at[:, rows], adj_buf.at[block], sem.at[block, 0]),
            pltpu.make_async_copy(vel.at[:, :, rows], vel_buf.at[block], sem.at[block, 1]),
            pltpu.make_async_copy(kap.at[:, rows], kap_buf.at[block], sem.at[block, 2]),
        ]

    @pl.when(at == 0)
    def _():
        for block in range(blocks):
            for copy in copies(block):
                copy.start()

    for copy in copies(at):
        copy.wait()
    adj, vel, kap = adj_buf.at[at], vel_buf.at[at], kap_buf.at[at]

    def each(partner, other, l):
        odd = odd_tile()
        ws = [wide(adj[f, l]) for f in range(FIELDS)]
        sent = []
        for s in (1, 0):
            r = rates(wide(vel[s, 0, l]), wide(vel[s, 1, l]), wide(kap[s, l]))
            out = leaving_rates({k: ends(v) for k, v in r.items() if k in ("down", "up", "far")})
            sent.append(leaving([ends(w) for w in ws], out))
            r = inside(r, 0, LON - 1)
            ws = [step(w, r) for w in ws]
        sent.append(leaving_rows(out))
        put_message(partner, l, *[jnp.where(odd, p, n) for n, p in sent])
        put_message(other, l, *[jnp.where(odd, n, p) for n, p in sent])
        put_packed(mid, l, [middle(w) for w in ws])
        for f, w in enumerate(ws):
            image[l, f] = ends(w)

    if len(messages) == 2:
        levels(functools.partial(each, *messages))
    else:

        @pl.when(at < SPLIT // BLOCK)
        def _():
            levels(functools.partial(each, *messages[:2]))

        @pl.when(at >= SPLIT // BLOCK)
        def _():
            levels(functools.partial(each, *messages[2:]))


def second_kernel(vel, kap, partner, other, from_partner, from_other, image, *refs):
    packed = refs[-1]

    @levels
    def _(l):
        odd = odd_tile()
        row = lax.broadcasted_iota(jnp.int32, (8, WIDE), 0)
        even_row = row % 2 == 0
        sides = []
        for (mine_even, mine_odd), (theirs_even, theirs_odd) in (
            ((other, partner), (from_other, from_partner)),
            ((partner, other), (from_partner, from_other)),
        ):
            mine = jnp.where(odd, mine_odd[l], mine_even[l])
            theirs = jnp.where(odd, theirs_odd[l], theirs_even[l])
            sides.append((get_tile(mine, 0), get_tile(theirs, 0), get_tile(theirs, 1), theirs))
        gave, low, low_then, theirs = sides[0]
        low_then += jnp.where(even_row, get_rate(theirs, 0), get_rate(theirs, 1)) * gave
        low_then += jnp.where(even_row, get_rate(theirs, 2) * rolled(gave, -1, 0), 0.0)
        gave, high, high_then, theirs = sides[1]
        high_then -= jnp.where(even_row, get_rate(theirs, 0), get_rate(theirs, 1)) * gave
        high_then += jnp.where(even_row, 0.0, get_rate(theirs, 2) * rolled(gave, 1, 0))
        r = rates(wide(ends(vel[0, 0, l])), wide(ends(vel[0, 1, l])), wide(ends(kap[0, l])))
        r = inside(r, 0, 7)
        pieces = []
        for f in range(FIELDS):
            new = arriving(low, high, f)
            pieces.append(image[l, f] + step(new, r) + arriving(low_then, high_then, f))
        put_packed(packed, l, pieces)


def last_kernel(direct, adj, end, mid, *refs):
    out = refs[-1]
    win, windows = lax.axis_index("win"), lax.axis_size("win")
    late, none = win == windows // 2 - 1, win == windows - 1
    mid_late = refs[0] if direct else None
    row = lax.broadcasted_iota(jnp.int32, (8, 128), 0)

    @levels
    def _(l):
        for f in range(FIELDS):
            for part in range(3):
                lanes = slice(128 * part, min(128 * part + 128, LAT))
                n = lanes.stop - lanes.start
                m, e = get_packed(mid, l, f, part), get_packed(end, l, f, part)
                if direct:
                    m = jnp.where(late, get_packed(mid_late, l, f, part), jnp.where(none, 0.0, m))
                out[f, l, 0:8, lanes] = adj[f, l, 0:8, lanes] - jnp.where(row < 4, e, m)[:, :n]
                out[f, l, 8:16, lanes] = adj[f, l, 8:16, lanes] - jnp.where(row < 4, m, e)[:, :n]


def spec(dims, at, first=0):
    block = tuple(BLOCK if i == at else d for i, d in enumerate(dims))
    return pl.BlockSpec(block, lambda i: tuple(first + i if k == at else 0 for k in range(len(dims))))


def part_spec(begin, end):
    return pl.BlockSpec((BLOCK, *MESSAGE[1:]), lambda i: (jnp.clip(i - begin, 0, end - begin - 1), 0, 0))


def f32(*dims):
    return jax.ShapeDtypeStruct(dims, jnp.float32)


def call(flops, kernel, count, in_specs, out_specs, out_shape, name, args, after=(), into=(), scratch=(), vmem=24):
    args, in_specs, aliases = list(args), list(in_specs), {}
    for extra in after:
        args.append(extra)
        in_specs.append(pl.BlockSpec(memory_space=pl.ANY))
    for k, buffer in enumerate(into):
        if buffer is not None:
            aliases[len(args)] = k
            args.append(buffer)
            in_specs.append(pl.BlockSpec(memory_space=pl.ANY))
    return pl.pallas_call(
        kernel,
        grid=(count // BLOCK,),
        in_specs=in_specs,
        out_specs=out_specs,
        out_shape=out_shape,
        scratch_shapes=list(scratch),
        name=name,
        input_output_aliases=aliases,
        cost_estimate=pl.CostEstimate(flops=flops, bytes_accessed=1, transcendentals=0),
        compiler_params=pltpu.CompilerParams(vmem_limit_bytes=vmem * MIB),
    )(*args)


MESSAGE = (0, 48, 128)
FIELD_TILES = (0, FIELDS, 8, WIDE)
PACKED = (0, 80, 128)


def sized(dims, n):
    return f32(n, *dims[1:])


def swapped(partner, other):
    n = lax.axis_size("tile")
    inner = [(i, i ^ 1) for i in range(n)]
    outer = [(i, (i + 1 if i % 2 else i - 1) % n) for i in range(n)]
    return lax.ppermute(partner, "tile", inner), lax.ppermute(other, "tile", outer)


def to_preceding(x):
    n = lax.axis_size("win")
    return lax.ppermute(x, "win", [(k + 1, k) for k in range(n - 1)])


def detour(x, step):
    n = lax.axis_size("win")
    if step:
        return lax.ppermute(x, "win", [(n - 1, n // 2 - 1)])
    return lax.ppermute(x, "win", [(k + 1, n - 1 if k + 1 == n // 2 else k) for k in range(n - 1)])


def long_way(x, step):
    n = lax.axis_size("win")
    h = n // 2
    side = ((h, h + 1), (h + 1, 2), (2, 3))[step]
    pairs = [(g + s, g + (s + 1) % h) for g in (0, h) for s in range(h) if s != step]
    return lax.ppermute(x, "win", [*pairs, side])


def per_device(adjoint, velocity, kappa):
    adj, vel, kap = adjoint[0], velocity[0], kappa[0]
    scratch = [
        (FIELDS, BLOCK, LON, LAT),
        (2, 2, BLOCK, LON, LAT),
        (2, BLOCK, LON, LAT),
    ]
    groups, after = [], []
    cut, rest = SPLIT // BLOCK, sized(MESSAGE, sum(n for _, n, _ in GROUPS) - SPLIT)
    early = late = None
    for start, n, around in GROUPS:
        blocks = n // BLOCK
        if early is None:
            specs = [part_spec(0, cut)] * 2 + [part_spec(cut, blocks)] * 2
            shapes, into = [sized(MESSAGE, SPLIT)] * 2 + [rest] * 2, ()
        else:
            specs = [spec(MESSAGE, 0, (start - SPLIT) // BLOCK)] * 2
            shapes, into = [rest] * 2, (None, None, *late)
        mid, image, *mine = call(
            FLOPS[0], functools.partial(first_kernel, start, blocks, 2 + len(specs)), n,
            [pl.BlockSpec(memory_space=pltpu.HBM)] * 3,
            [spec(d, 0) for d in (PACKED, FIELD_TILES)] + specs,
            [sized(d, n) for d in (PACKED, FIELD_TILES)] + shapes,
            "interior", (adj, vel, kap), after, into,
            [pltpu.VMEM((blocks, *d), jnp.float32) for d in scratch] + [pltpu.SemaphoreType.DMA((blocks, 3))],
            FIRST_VMEM,
        )
        after = [mid]
        if early is None:
            early = mine[:2]
            early_theirs = swapped(*early)
        late = mine[-2:]
        groups.append(([(long_way if around else detour)(mid, 0)], image))
    exchanges = ((early, early_theirs), (late, swapped(*late)))
    lasts, after = [], []
    for k, (first, count, group, exchange) in enumerate(ENDS):
        mine, theirs = exchanges[exchange]
        b = first // BLOCK
        c, m = (first - GROUPS[group][0]) // BLOCK, (first - SPLIT * exchange) // BLOCK
        if k == 1:
            after = [*after, groups[1][0][0]]
        end = call(
            FLOPS[1], second_kernel, count,
            [spec((1, *vel.shape[1:]), 2, b), spec((1, *kap.shape[1:]), 1, b)]
            + [spec(MESSAGE, 0, m)] * 4 + [spec(FIELD_TILES, 0, c)],
            spec(PACKED, 0), sized(PACKED, count), "ends", (vel, kap, *mine, *theirs, groups[group][1]), after,
        )
        after = [end]
        lasts.append(to_preceding(end))
        for at, (mid, _), (_, _, around) in zip(STEPS, groups, GROUPS):
            if k in at:
                x = lax.optimization_barrier([mid[-1], end])[0]
                mid.append((long_way if around else detour)(x, len(mid)))
    out, after = None, [end]
    for (first, count, group, _), end in zip(ENDS, lasts):
        b = first // BLOCK
        mid, around = groups[group][0], GROUPS[group][2]
        arrays = (adj, end, mid[-1]) if around else (adj, end, *mid)
        c = (first - GROUPS[group][0]) // BLOCK
        out = call(
            FLOPS[2], functools.partial(last_kernel, not around), count,
            [spec(adj.shape, 1, b), spec(PACKED, 0)] + [spec(PACKED, 0, c)] * (len(arrays) - 2),
            spec(adj.shape, 1, b), f32(*adj.shape), "subtract", arrays, after, [out],
        )
        after = []
    return out[None]


def solution(mesh):
    return jax.shard_map(
        per_device,
        mesh=mesh,
        in_specs=(
            P("win", None, None, "tile", None),
            P("win", None, None, None, "tile", None),
            P("win", None, None, "tile", None),
        ),
        out_specs=P("win", None, None, "tile", None),
        check_vma=False,
    )
```
